32 devices in a mesh: band: 4 (over x, core), row: 4 (over z), col: 2 (over y).
Axes of the slice: x: 2, y: 2, z: 4, core: 2. Of those that a mesh axis runs over, the one named last changes fastest.
Arguments:
- tokens: bfloat16 [256, 4, 16, 1024], P(('band', 'row'), 'col'), may hold values from -10 to 10
- counts: int32 [4], replicated, may hold values from 1 to 4, as said below
- norm_band: bfloat16 [1024], replicated, may hold values from 0.099609375 to 1.8984375
- w_band_qkv: bfloat16 [1024, 1536], replicated, may hold values from -1 to 1
- w_band_out: bfloat16 [512, 1024], replicated, may hold values from -0.25 to 0.25
- norm_space: bfloat16 [1024], replicated, may hold values from 0.099609375 to 1.8984375
- w_space_qkv: bfloat16 [1024, 1536], replicated, may hold values from -1 to 1
- w_space_out: bfloat16 [512, 1024], replicated, may hold values from -0.25 to 0.25
Outputs:
- layer_out: bfloat16 [256, 4, 16, 1024], P(('band', 'row'), 'col')
The draws below stay inside these ranges and needn't reach their ends.
Inputs may be any that keep to these rules, and one draw needn't show every extreme that they name: `counts`: every group holds at least one live token; some group is full and some group holds exactly one.
All inputs are finite; a program needn't handle non-finite values.
Results may differ from the reference program's by a relative error of at most 0.0063.
Values may be sent and summed in bfloat16 or wider, within the bound.
A program may use at most 128 MiB of HBM per device.

```python
import math
import jax
import jax.numpy as jnp
from jax import lax

D = 1024
HD = 64
HB = 8
HR = 4
HC = 4
BGROUPS = 4
BCAP = 4
NR = 256
NC = 4
BS = 16


def draw_tokens(key, part):
    base = jax.random.normal(jax.random.fold_in(key, 1), (NR, NC, BS, D), jnp.float32)
    return jnp.clip(base, -10.0, 10.0).astype(jnp.bfloat16)


def spiked_weight(key, salt, heads):
    weights = jax.random.normal(jax.random.fold_in(key, salt), (D, 3 * heads * HD), jnp.float32) / math.sqrt(D)
    return jnp.clip(weights, -1.0, 1.0)


def draw_w_band_qkv(key, part):
    return spiked_weight(key, 11, HB).astype(jnp.bfloat16)


def draw_w_space_qkv(key, part):
    return spiked_weight(key, 21, HR + HC).astype(jnp.bfloat16)


def draw_counts(key, part):
    drawn = jax.random.randint(jax.random.fold_in(key, 5), (BGROUPS,), 1, BCAP + 1)
    fullest = jax.random.randint(jax.random.fold_in(key, 6), (), 0, BGROUPS)
    offset = jax.random.randint(jax.random.fold_in(key, 7), (), 1, BGROUPS)
    sparsest = (fullest + offset) % BGROUPS
    groups = jnp.arange(BGROUPS)
    drawn = jnp.where(groups == sparsest, 1, drawn)
    return jnp.where(groups == fullest, BCAP, drawn).astype(jnp.int32)


def noise(key, dims, spread, limit, kind=jnp.bfloat16):
    result = spread * jax.random.normal(key, dims, jnp.float32)
    return jnp.clip(result, min=-limit, max=limit).astype(kind)


def setup_inputs(seed: int = 0) -> dict:
    splits = jax.random.split(jax.random.key(seed), 9)
    return {
        "tokens": draw_tokens(jax.random.fold_in(splits[8], 71), 0),
        "counts": draw_counts(jax.random.fold_in(splits[8], 71), 0),
        "norm_band": jnp.clip(1.0 + 0.18 * jax.random.normal(splits[2], (D,), jnp.float32), 0.099609375, 1.8984375).astype(jnp.bfloat16),
        "w_band_qkv": draw_w_band_qkv(jax.random.fold_in(splits[8], 71), 0),
        "w_band_out": noise(splits[4], (HB * HD, D), (HB * HD) ** -0.5, 0.25),
        "norm_space": jnp.clip(1.0 + 0.18 * jax.random.normal(splits[5], (D,), jnp.float32), 0.099609375, 1.8984375).astype(jnp.bfloat16),
        "w_space_qkv": draw_w_space_qkv(jax.random.fold_in(splits[8], 71), 0),
        "w_space_out": noise(splits[7], ((HR + HC) * HD, D), ((HR + HC) * HD) ** -0.5, 0.25),
    }


EPS = 1e-06

def rms_norm(values, gain):
    wide = values.astype(jnp.float32)
    scale = lax.rsqrt(lax.optimization_barrier(jnp.mean(wide * wide, axis=-1, keepdims=True)) + EPS)
    return (wide * scale * gain.astype(jnp.float32)).astype(jnp.bfloat16)

def widen(values):
    return lax.optimization_barrier(values.astype(jnp.bfloat16)).astype(jnp.float32)

def band_rows(token_row, live, norm_band, w_band_qkv, w_band_out, norm_space, w_space_qkv):
    normed = rms_norm(token_row, norm_band)
    qkv = widen(jnp.dot(normed.reshape(-1, D), w_band_qkv, preferred_element_type=jnp.float32))
    qkv = qkv.reshape(NC, BS, 3, HB, HD)
    scores = jnp.einsum('pihd,pjhd->phij', qkv[:, :, 0], qkv[:, :, 1]) * HD ** (-0.5)
    scores = jnp.where(live[None, None, None, :], scores, -1e+30)
    top = lax.optimization_barrier(jnp.max(scores, axis=-1, keepdims=True))
    probs = jnp.exp(scores - top)
    total = lax.optimization_barrier(jnp.sum(probs, axis=-1))
    mixed = jnp.einsum('phij,pjhd->pihd', widen(probs), qkv[:, :, 2])
    mixed = mixed / jnp.transpose(total, (0, 2, 1))[..., None]
    heads_out = mixed.astype(jnp.bfloat16).reshape(NC * BS, HB * HD)
    resid = token_row.astype(jnp.float32) + jnp.dot(heads_out, w_band_out, preferred_element_type=jnp.float32).reshape(NC, BS, D)
    normed2 = rms_norm(resid, norm_space)
    space_qkv = jnp.dot(normed2.reshape(-1, D), w_space_qkv, preferred_element_type=jnp.float32).astype(jnp.bfloat16)
    return (resid, space_qkv.reshape(NC, BS, 3, HR + HC, HD))

def axial(block, first, last):
    query = widen(block[:, :, 0, first:last])
    keys = widen(block[:, :, 1, first:last])
    vals = widen(block[:, :, 2, first:last])
    scores = jnp.einsum('ishd,jshd->shij', query, keys) * HD ** (-0.5)
    top = lax.optimization_barrier(jnp.max(scores, axis=-1, keepdims=True))
    probs = jnp.exp(scores - top)
    total = lax.optimization_barrier(jnp.sum(probs, axis=-1))
    mixed = jnp.einsum('shij,jshd->ishd', widen(probs), vals)
    mixed = mixed / jnp.transpose(total, (2, 0, 1))[..., None]
    return mixed.astype(jnp.bfloat16)

def reference(tokens, counts, norm_band, w_band_qkv, w_band_out, norm_space, w_space_qkv, w_space_out):
    slots = jnp.arange(BS, dtype=jnp.int32)
    live = slots % BCAP < counts[slots // BCAP]
    resid, space_qkv = lax.map(lambda token_row: band_rows(token_row, live, norm_band, w_band_qkv, w_band_out, norm_space, w_space_qkv), tokens)
    row_heads = lax.map(lambda block: axial(block, 0, HR), space_qkv)
    col_heads = lax.map(lambda block: axial(block, HR, HR + HC), jnp.swapaxes(space_qkv, 0, 1))
    col_heads = jnp.swapaxes(col_heads, 0, 1)
    heads = jnp.concatenate([row_heads.reshape(NR, NC, BS, HR * HD), col_heads.reshape(NR, NC, BS, HC * HD)], axis=-1)

    def finish(pair):
        resid_row, heads_row = pair
        mixed = jnp.dot(heads_row.reshape(NC * BS, (HR + HC) * HD), w_space_out, preferred_element_type=jnp.float32)
        return (resid_row + mixed.reshape(NC, BS, D)).astype(jnp.bfloat16)
    return lax.map(finish, (resid, heads))
```

```python
import functools

import jax
import jax.numpy as jnp
from jax import lax
from jax.experimental import pallas as pl
from jax.experimental.pallas import tpu as pltpu
from jax.sharding import PartitionSpec as P

HD = 64
HB = 8
HR = 4
HC = 4


EPS = 1e-06
LOG2E = 1.4426950408889634
MESH = pl.DeviceIdType.MESH
PAIR = 2 * HD


def rms_norm(wide, gain):
    scale = lax.rsqrt(jnp.mean(wide * wide, axis=-1, keepdims=True) + EPS)
    return (wide * scale * gain).astype(jnp.bfloat16)


def dot(left, right):
    return jnp.dot(left, right, preferred_element_type=jnp.float32)


def lane_masks():
    first = lax.broadcasted_iota(jnp.int32, (1, PAIR), 1) < HD
    wide = jnp.where(first, 1.0, 0.0)
    return first, wide.astype(jnp.bfloat16), (1.0 - wide).astype(jnp.bfloat16)


def attend(q, k, v, bias):
    first, even, odd = lane_masks()
    m = k.shape[0]
    keys = jnp.concatenate([k * even, k * odd], axis=0)
    vals = jnp.concatenate([v * even, v * odd], axis=0)
    scores = lax.dot_general(
        q, keys, (((1,), (1,)), ((), ())), preferred_element_type=jnp.float32
    )
    probs, totals = [], []
    for h in range(2):
        part = scores[:, h * m : (h + 1) * m] * (HD ** (-0.5) * LOG2E)
        if bias is not None:
            part = part + bias
        part = jnp.exp2(part - jnp.max(part, axis=-1, keepdims=True))
        totals.append(jnp.sum(part, axis=-1, keepdims=True))
        probs.append(part.astype(jnp.bfloat16))
    mixed = dot(jnp.concatenate(probs, axis=1), vals)
    return (mixed / jnp.where(first, totals[0], totals[1])).astype(jnp.bfloat16)


def kernel(
    sizes,
    counts_ref, nb_ref, ns_ref, tok_hbm, wbq_hbm, wbo_hbm, wsq_hbm, wso_hbm,
    out_hbm,
    tok, wbq, wbo, wsq, wso, resid, qkv, heads, perm, perm_back, band_bias, row_bias,
    col_send, col_recv, col_out, col_ret, row_send, row_recv, row_out, row_ret, outv,
    load_sem, out_sem, cfs, cfr, crs, crr, rfs, rfr, rrs, rrr,
):
    nband, nrow, ncol, prows, pcols, slots, groups = sizes
    many = nband * nrow
    width = tok.shape[-1]
    n = prows * slots
    share = slots // many
    lines = prows // ncol
    band, row, col = (lax.axis_index(a) for a in ("band", "row", "col"))
    me = band * nrow + row

    def along(d):
        peer = lax.rem(me + d, many)
        return peer, (lax.div(peer, nrow), lax.rem(peer, nrow), col)

    def across(d):
        peer = lax.rem(col + d, ncol)
        return peer, (band, row, peer)

    barrier = pltpu.get_barrier_semaphore()
    for d in range(1, many):
        pl.semaphore_signal(barrier, inc=1, device_id=along(d)[1], device_id_type=MESH)
    for d in range(1, ncol):
        pl.semaphore_signal(barrier, inc=1, device_id=across(d)[1], device_id_type=MESH)

    loads = [pltpu.make_async_copy(tok_hbm.at[:, c], tok.at[c], load_sem.at[c]) for c in range(pcols)]
    pairs = ((wbq_hbm, wbq), (wbo_hbm, wbo), (wsq_hbm, wsq), (wso_hbm, wso))
    weights = [pltpu.make_async_copy(a, b, load_sem.at[pcols + i]) for i, (a, b) in enumerate(pairs)]
    loads[0].start()
    weights[0].start()
    for copy in loads[1:] + weights[1:]:
        copy.start()

    at = lax.broadcasted_iota(jnp.int32, (n, n), 0)
    to = lax.broadcasted_iota(jnp.int32, (n, n), 1)
    perm[...] = jnp.where(
        lax.rem(at, prows) * slots + lax.div(at, prows) == to, 1.0, 0.0
    ).astype(jnp.bfloat16)
    perm_back[...] = jnp.where(
        lax.rem(to, prows) * slots + lax.div(to, prows) == at, 1.0, 0.0
    ).astype(jnp.bfloat16)
    nblock = band_bias.shape[0]
    at = lax.broadcasted_iota(jnp.int32, (nblock, nblock), 0)
    to = lax.broadcasted_iota(jnp.int32, (nblock, nblock), 1)
    slot = lax.rem(to, slots)
    cap = slots // groups
    group = lax.div(slot, cap)
    limit = jnp.zeros_like(slot)
    for g in range(groups):
        limit = jnp.where(group == g, counts_ref[g], limit)
    keep = jnp.logical_and(
        lax.div(at, slots) == lax.div(to, slots), lax.rem(slot, cap) < limit
    )
    band_bias[...] = jnp.where(keep, 0.0, -1e30)
    rblock = row_bias.shape[0]
    unit = rblock // (ncol * pcols)
    at = lax.broadcasted_iota(jnp.int32, (rblock, rblock), 0)
    to = lax.broadcasted_iota(jnp.int32, (rblock, rblock), 1)
    row_bias[...] = jnp.where(lax.rem(at, unit) == lax.rem(to, unit), 0.0, -1e30)

    gain_band = nb_ref[...].astype(jnp.float32)
    gain_space = ns_ref[...].astype(jnp.float32)
    bw = HB * HD
    rw, cw = HR * HD, HC * HD
    sw = rw + cw
    col_fwd, row_fwd = [], []
    for c in range(pcols):
        loads[c].wait()
        x = tok[c].reshape(n, width).astype(jnp.float32)
        normed = rms_norm(x, gain_band)
        if c == 0:
            weights[0].wait()
        qkv[...] = dot(normed, wbq[...]).astype(jnp.bfloat16)
        for b in range(n // nblock):
            rows = slice(b * nblock, (b + 1) * nblock)
            for p in range(bw // PAIR):
                q, k, v = (
                    qkv[rows, t * bw + p * PAIR : t * bw + (p + 1) * PAIR] for t in range(3)
                )
                heads[rows, p * PAIR : (p + 1) * PAIR] = attend(q, k, v, band_bias[...])
        if c == 0:
            weights[1].wait()
        x = tok[c].reshape(n, width).astype(jnp.float32) + dot(heads[...], wbo[...])
        resid[c] = x
        normed = rms_norm(x, gain_space)
        if c == 0:
            weights[2].wait()
        for t in range(3):
            part = dot(normed, wsq[:, t * sw + rw : (t + 1) * sw]).astype(jnp.bfloat16)
            part = dot(perm[...], part).astype(jnp.bfloat16)
            col_send[c, :, :, t * cw : (t + 1) * cw] = part.reshape(many, share * prows, cw)
        if c == 0:
            pl.semaphore_wait(barrier, many - 1 + ncol - 1)
        fwd = []
        for d in range(1, many):
            peer, device = along(d)
            copy = pltpu.make_async_remote_copy(
                src_ref=col_send.at[c, peer],
                dst_ref=col_recv.at[c, me],
                send_sem=cfs.at[c, d],
                recv_sem=cfr.at[c, d],
                device_id=device,
                device_id_type=MESH,
            )
            copy.start()
            fwd.append(copy)
        col_fwd.append(fwd)
        for t in range(3):
            part = dot(normed, wsq[:, t * sw : t * sw + rw]).astype(jnp.bfloat16)
            row_send[c, :, :, t * rw : (t + 1) * rw] = part.reshape(ncol, lines * slots, rw)
        fwd = []
        for d in range(1, ncol):
            peer, device = across(d)
            copy = pltpu.make_async_remote_copy(
                src_ref=row_send.at[c, peer],
                dst_ref=row_recv.at[col * pcols + c],
                send_sem=rfs.at[c, d],
                recv_sem=rfr.at[c, d],
                device_id=device,
                device_id_type=MESH,
            )
            copy.start()
            fwd.append(copy)
        row_fwd.append(fwd)
        col_recv[c, me] = col_send[c, me]
        row_recv[col * pcols + c] = row_send[c, col]

    col_bwd, row_bwd = [], []

    def do_col(c):
        for copy in col_fwd[c]:
            copy.wait_recv()
        for s in range(share):
            rows = slice(s * prows, (s + 1) * prows)
            for p in range(cw // PAIR):
                q, k, v = (
                    col_recv[c, :, rows, t * cw + p * PAIR : t * cw + (p + 1) * PAIR].reshape(
                        many * prows, PAIR
                    )
                    for t in range(3)
                )
                col_out[c, :, rows, p * PAIR : (p + 1) * PAIR] = attend(q, k, v, None).reshape(
                    many, prows, PAIR
                )
        back = []
        for d in range(1, many):
            peer, device = along(d)
            copy = pltpu.make_async_remote_copy(
                src_ref=col_out.at[c, peer],
                dst_ref=col_ret.at[c, me],
                send_sem=crs.at[c, d],
                recv_sem=crr.at[c, d],
                device_id=device,
                device_id_type=MESH,
            )
            copy.start()
            back.append(copy)
        col_bwd.append(back)
        col_ret[c, me] = col_out[c, me]

    def do_row():
        for fwd in row_fwd:
            for copy in fwd:
                copy.wait_recv()
        for b in range(lines * slots // unit):
            rows = slice(b * unit, (b + 1) * unit)
            for p in range(rw // PAIR):
                q, k, v = (
                    row_recv[:, rows, t * rw + p * PAIR : t * rw + (p + 1) * PAIR].reshape(
                        rblock, PAIR
                    )
                    for t in range(3)
                )
                row_out[:, rows, p * PAIR : (p + 1) * PAIR] = attend(
                    q, k, v, row_bias[...]
                ).reshape(ncol * pcols, unit, PAIR)
        for d in range(1, ncol):
            peer, device = across(d)
            copy = pltpu.make_async_remote_copy(
                src_ref=row_out.at[pl.ds(peer * pcols, pcols)],
                dst_ref=row_ret.at[col],
                send_sem=rrs.at[d],
                recv_sem=rrr.at[d],
                device_id=device,
                device_id_type=MESH,
            )
            copy.start()
            row_bwd.append(copy)
        row_ret[col] = row_out[pl.ds(col * pcols, pcols)]

    do_col(0)
    do_row()
    for c in range(1, pcols):
        do_col(c)

    weights[3].wait()
    for copy in row_bwd:
        copy.wait_recv()
    stores = []
    for c in range(pcols):
        acc = resid[c] + dot(row_ret[:, c].reshape(n, rw), wso[:rw, :])
        for copy in col_bwd[c]:
            copy.wait_recv()
        part = dot(perm_back[...], col_ret[c].reshape(n, cw)).astype(jnp.bfloat16)
        acc = acc + dot(part, wso[rw:, :])
        outv[c] = acc.astype(jnp.bfloat16).reshape(prows, slots, width)
        store = pltpu.make_async_copy(outv.at[c], out_hbm.at[:, c], out_sem.at[c])
        store.start()
        stores.append(store)
    for copies in col_fwd + row_fwd + col_bwd + [row_bwd]:
        for copy in copies:
            copy.wait_send()
    for store in stores:
        store.wait()


def local(mesh_sizes, tokens, counts, norm_band, w_band_qkv, w_band_out, norm_space, w_space_qkv, w_space_out):
    nband, nrow, ncol = mesh_sizes
    prows, pcols, slots, width = tokens.shape
    many = nband * nrow
    n = prows * slots
    share, lines = slots // many, prows // ncol
    cols = ncol * pcols
    bands = max(1, 128 // slots) * slots
    while n % bands:
        bands -= slots
    unit = max(1, min(lines, 128 // (cols * slots)))
    while lines % unit:
        unit -= 1
    rblock = cols * unit * slots
    rw, cw = HR * HD, HC * HD
    bf16, f32 = jnp.bfloat16, jnp.float32
    vmem = pltpu.VMEM
    dma = pltpu.SemaphoreType.DMA
    sizes = (nband, nrow, ncol, prows, pcols, slots, counts.shape[0])
    anywhere = pl.BlockSpec(memory_space=pl.ANY)
    whole = pl.BlockSpec(memory_space=pltpu.VMEM)
    return pl.pallas_call(
        functools.partial(kernel, sizes),
        out_shape=jax.ShapeDtypeStruct(tokens.shape, bf16),
        in_specs=[pl.BlockSpec(memory_space=pltpu.SMEM), whole, whole] + [anywhere] * 5,
        out_specs=anywhere,
        scratch_shapes=[
            vmem((pcols, prows, slots, width), bf16),
            vmem(w_band_qkv.shape, bf16),
            vmem(w_band_out.shape, bf16),
            vmem(w_space_qkv.shape, bf16),
            vmem(w_space_out.shape, bf16),
            vmem((pcols, n, width), f32),
            vmem((n, 3 * HB * HD), bf16),
            vmem((n, HB * HD), bf16),
            vmem((n, n), bf16),
            vmem((n, n), bf16),
            vmem((bands, bands), f32),
            vmem((rblock, rblock), f32),
            vmem((pcols, many, share * prows, 3 * cw), bf16),
            vmem((pcols, many, share * prows, 3 * cw), bf16),
            vmem((pcols, many, share * prows, cw), bf16),
            vmem((pcols, many, share * prows, cw), bf16),
            vmem((pcols, ncol, lines * slots, 3 * rw), bf16),
            vmem((cols, lines * slots, 3 * rw), bf16),
            vmem((cols, lines * slots, rw), bf16),
            vmem((ncol, pcols, lines * slots, rw), bf16),
            vmem((pcols, prows, slots, width), bf16),
            dma((pcols + 4,)),
            dma((pcols,)),
            dma((pcols, many)),
            dma((pcols, many)),
            dma((pcols, many)),
            dma((pcols, many)),
            dma((pcols, ncol)),
            dma((pcols, ncol)),
            dma((ncol,)),
            dma((ncol,)),
        ],
        compiler_params=pltpu.CompilerParams(
            collective_id=0, has_side_effects=True, vmem_limit_bytes=48 * 1024 * 1024
        ),
        cost_estimate=pl.CostEstimate(
            flops=12 * prows * pcols * slots * width * width // 2,
            bytes_accessed=12 * 1024 * 1024,
            transcendentals=4 * 1024 * 1024,
        ),
    )(
        counts,
        norm_band.reshape(1, -1),
        norm_space.reshape(1, -1),
        tokens,
        w_band_qkv,
        w_band_out,
        w_space_qkv,
        w_space_out,
    )


def solution(mesh):
    sizes = tuple(mesh.shape[a] for a in ("band", "row", "col"))
    placed = (P(("band", "row"), "col", None, None), P(), P(), P(), P(), P(), P(), P())
    return jax.shard_map(
        functools.partial(local, sizes),
        mesh=mesh,
        in_specs=placed,
        out_specs=P(("band", "row"), "col", None, None),
        check_vma=False,
    )
```

```python
import functools

import jax
import jax.numpy as jnp
from jax import lax
from jax.experimental import pallas as pl
from jax.experimental.pallas import tpu as pltpu
from jax.sharding import PartitionSpec as P

HD = 64
HB = 8
HR = 4
HC = 4


EPS = 1e-06
LOG2E = 1.4426950408889634
MESH = pl.DeviceIdType.MESH
PAIR = 2 * HD
LIMIT = 63 * 1024 * 1024


def rms_norm(wide, gain):
    scale = lax.rsqrt(jnp.mean(wide * wide, axis=-1, keepdims=True) + EPS)
    return (wide * scale * gain).astype(jnp.bfloat16)


def dot(left, right):
    return jnp.dot(left, right, preferred_element_type=jnp.float32)


def lane_masks():
    first = lax.broadcasted_iota(jnp.int32, (1, PAIR), 1) < HD
    wide = jnp.where(first, 1.0, 0.0)
    return first, wide.astype(jnp.bfloat16), (1.0 - wide).astype(jnp.bfloat16)


def attend(q, k, v, bias):
    first, even, odd = lane_masks()
    m = k.shape[0]
    keys = jnp.concatenate([k * even, k * odd], axis=0)
    vals = jnp.concatenate([v * even, v * odd], axis=0)
    scores = lax.dot_general(
        q, keys, (((1,), (1,)), ((), ())), preferred_element_type=jnp.float32
    )
    probs, totals = [], []
    for h in range(2):
        part = scores[:, h * m : (h + 1) * m] * (HD ** (-0.5) * LOG2E)
        if bias is not None:
            part = part + bias
        part = jnp.exp2(part - jnp.max(part, axis=-1, keepdims=True))
        totals.append(jnp.sum(part, axis=-1, keepdims=True))
        probs.append(part.astype(jnp.bfloat16))
    mixed = dot(jnp.concatenate(probs, axis=1), vals)
    return (mixed / jnp.where(first, totals[0], totals[1])).astype(jnp.bfloat16)


def kernel(
    sizes,
    counts_hbm, nb_hbm, ns_hbm, tok_hbm, wbq_hbm, wbo_hbm, wsq_hbm, wso_hbm,
    out_hbm,
    tok, wbq, wbo, wsq, wso, resid, qkv, heads, perm, perm_back, band_bias, row_bias,
    col_send, col_recv, col_out, col_ret, row_send, row_recv, row_out, row_ret, outv,
    counts_ref, nb_ref, ns_ref, load_sem, out_sem, cfs, cfr, crs, crr, rfs, rfr, rrs, rrr,
):
    nband, nrow, ncol, prows, pcols, slots, groups = sizes
    many = nband * nrow
    width = tok.shape[-1]
    n = prows * slots
    share = slots // many
    lines = prows // ncol
    band, row, col = (lax.axis_index(a) for a in ("band", "row", "col"))
    me = band * nrow + row

    def along(d):
        peer = lax.rem(me + d, many)
        return peer, (lax.div(peer, nrow), lax.rem(peer, nrow), col)

    def across(d):
        peer = lax.rem(col + d, ncol)
        return peer, (band, row, peer)

    barrier = pltpu.get_barrier_semaphore()
    for d in range(1, many):
        pl.semaphore_signal(barrier, inc=1, device_id=along(d)[1], device_id_type=MESH)
    for d in range(1, ncol):
        pl.semaphore_signal(barrier, inc=1, device_id=across(d)[1], device_id_type=MESH)

    loads = [pltpu.make_async_copy(tok_hbm.at[:, c], tok.at[c], load_sem.at[c]) for c in range(pcols)]
    pairs = ((wbq_hbm, wbq), (wbo_hbm, wbo), (wsq_hbm, wsq), (wso_hbm, wso))
    weights = [pltpu.make_async_copy(a, b, load_sem.at[pcols + i]) for i, (a, b) in enumerate(pairs)]
    small = ((counts_hbm, counts_ref), (nb_hbm, nb_ref), (ns_hbm, ns_ref))
    small = [pltpu.make_async_copy(a, b, load_sem.at[pcols + 4 + i]) for i, (a, b) in enumerate(small)]
    loads[0].start()
    for copy in small:
        copy.start()
    weights[0].start()
    for copy in loads[1:] + weights[1:]:
        copy.start()

    at = lax.broadcasted_iota(jnp.int32, (n, n), 0)
    to = lax.broadcasted_iota(jnp.int32, (n, n), 1)
    perm[...] = jnp.where(
        lax.rem(at, prows) * slots + lax.div(at, prows) == to, 1.0, 0.0
    ).astype(jnp.bfloat16)
    perm_back[...] = jnp.where(
        lax.rem(to, prows) * slots + lax.div(to, prows) == at, 1.0, 0.0
    ).astype(jnp.bfloat16)
    for copy in small:
        copy.wait()
    nblock = band_bias.shape[0]
    at = lax.broadcasted_iota(jnp.int32, (nblock, nblock), 0)
    to = lax.broadcasted_iota(jnp.int32, (nblock, nblock), 1)
    slot = lax.rem(to, slots)
    cap = slots // groups
    group = lax.div(slot, cap)
    limit = jnp.zeros_like(slot)
    for g in range(groups):
        limit = jnp.where(group == g, counts_ref[g], limit)
    keep = jnp.logical_and(
        lax.div(at, slots) == lax.div(to, slots), lax.rem(slot, cap) < limit
    )
    band_bias[...] = jnp.where(keep, 0.0, -1e30)
    rblock = row_bias.shape[0]
    unit = rblock // (ncol * pcols)
    at = lax.broadcasted_iota(jnp.int32, (rblock, rblock), 0)
    to = lax.broadcasted_iota(jnp.int32, (rblock, rblock), 1)
    row_bias[...] = jnp.where(lax.rem(at, unit) == lax.rem(to, unit), 0.0, -1e30)

    gain_band = nb_ref[...].astype(jnp.float32).reshape(1, width)
    gain_space = ns_ref[...].astype(jnp.float32).reshape(1, width)
    bw = HB * HD
    rw, cw = HR * HD, HC * HD
    sw = rw + cw
    col_fwd, row_fwd = [], []
    for c in range(pcols):
        loads[c].wait()
        x = tok[c].reshape(n, width).astype(jnp.float32)
        normed = rms_norm(x, gain_band)
        if c == 0:
            weights[0].wait()
        qkv[...] = dot(normed, wbq[...]).astype(jnp.bfloat16)
        for b in range(n // nblock):
            rows = slice(b * nblock, (b + 1) * nblock)
            for p in range(bw // PAIR):
                q, k, v = (
                    qkv[rows, t * bw + p * PAIR : t * bw + (p + 1) * PAIR] for t in range(3)
                )
                heads[rows, p * PAIR : (p + 1) * PAIR] = attend(q, k, v, band_bias[...])
        if c == 0:
            weights[1].wait()
        x = tok[c].reshape(n, width).astype(jnp.float32) + dot(heads[...], wbo[...])
        resid[c] = x
        normed = rms_norm(x, gain_space)
        if c == 0:
            weights[2].wait()
        for t in range(3):
            part = dot(normed, wsq[:, t * sw + rw : (t + 1) * sw]).astype(jnp.bfloat16)
            part = dot(perm[...], part).astype(jnp.bfloat16)
            col_send[c, :, :, t * cw : (t + 1) * cw] = part.reshape(many, share * prows, cw)
        if c == 0:
            pl.semaphore_wait(barrier, many - 1 + ncol - 1)
        fwd = []
        for d in range(1, many):
            peer, device = along(d)
            copy = pltpu.make_async_remote_copy(
                src_ref=col_send.at[c, peer],
                dst_ref=col_recv.at[c, me],
                send_sem=cfs.at[c, d],
                recv_sem=cfr.at[c, d],
                device_id=device,
                device_id_type=MESH,
            )
            copy.start()
            fwd.append(copy)
        col_fwd.append(fwd)
        for t in range(3):
            part = dot(normed, wsq[:, t * sw : t * sw + rw]).astype(jnp.bfloat16)
            row_send[c, :, :, t * rw : (t + 1) * rw] = part.reshape(ncol, lines * slots, rw)
        fwd = []
        for d in range(1, ncol):
            peer, device = across(d)
            copy = pltpu.make_async_remote_copy(
                src_ref=row_send.at[c, peer],
                dst_ref=row_recv.at[col * pcols + c],
                send_sem=rfs.at[c, d],
                recv_sem=rfr.at[c, d],
                device_id=device,
                device_id_type=MESH,
            )
            copy.start()
            fwd.append(copy)
        row_fwd.append(fwd)
        col_recv[c, me] = col_send[c, me]
        row_recv[col * pcols + c] = row_send[c, col]

    col_bwd, row_bwd = [], []

    def do_col(c):
        for copy in col_fwd[c]:
            copy.wait_recv()
        for s in range(share):
            rows = slice(s * prows, (s + 1) * prows)
            for p in range(cw // PAIR):
                q, k, v = (
                    col_recv[c, :, rows, t * cw + p * PAIR : t * cw + (p + 1) * PAIR].reshape(
                        many * prows, PAIR
                    )
                    for t in range(3)
                )
                col_out[c, :, rows, p * PAIR : (p + 1) * PAIR] = attend(q, k, v, None).reshape(
                    many, prows, PAIR
                )
        back = []
        for d in range(1, many):
            peer, device = along(d)
            copy = pltpu.make_async_remote_copy(
                src_ref=col_out.at[c, peer],
                dst_ref=col_ret.at[c, me],
                send_sem=crs.at[c, d],
                recv_sem=crr.at[c, d],
                device_id=device,
                device_id_type=MESH,
            )
            copy.start()
            back.append(copy)
        col_bwd.append(back)
        col_ret[c, me] = col_out[c, me]

    def do_row():
        for fwd in row_fwd:
            for copy in fwd:
                copy.wait_recv()
        for b in range(lines * slots // unit):
            rows = slice(b * unit, (b + 1) * unit)
            for p in range(rw // PAIR):
                q, k, v = (
                    row_recv[:, rows, t * rw + p * PAIR : t * rw + (p + 1) * PAIR].reshape(
                        rblock, PAIR
                    )
                    for t in range(3)
                )
                row_out[:, rows, p * PAIR : (p + 1) * PAIR] = attend(
                    q, k, v, row_bias[...]
                ).reshape(ncol * pcols, unit, PAIR)
        for d in range(1, ncol):
            peer, device = across(d)
            copy = pltpu.make_async_remote_copy(
                src_ref=row_out.at[pl.ds(peer * pcols, pcols)],
                dst_ref=row_ret.at[col],
                send_sem=rrs.at[d],
                recv_sem=rrr.at[d],
                device_id=device,
                device_id_type=MESH,
            )
            copy.start()
            row_bwd.append(copy)
        row_ret[col] = row_out[pl.ds(col * pcols, pcols)]

    do_col(0)
    do_row()
    for c in range(1, pcols):
        do_col(c)

    weights[3].wait()
    for copy in row_bwd:
        copy.wait_recv()
    stores = []
    for c in range(pcols):
        acc = resid[c] + dot(row_ret[:, c].reshape(n, rw), wso[:rw, :])
        for copy in col_bwd[c]:
            copy.wait_recv()
        part = dot(perm_back[...], col_ret[c].reshape(n, cw)).astype(jnp.bfloat16)
        acc = acc + dot(part, wso[rw:, :])
        outv[c] = acc.astype(jnp.bfloat16).reshape(prows, slots, width)
        store = pltpu.make_async_copy(outv.at[c], out_hbm.at[:, c], out_sem.at[c])
        store.start()
        stores.append(store)
    for copies in col_fwd + row_fwd + col_bwd + [row_bwd]:
        for copy in copies:
            copy.wait_send()
    for store in stores:
        store.wait()


def local(mesh_sizes, tokens, counts, norm_band, w_band_qkv, w_band_out, norm_space, w_space_qkv, w_space_out):
    nband, nrow, ncol = mesh_sizes
    prows, pcols, slots, width = tokens.shape
    many = nband * nrow
    n = prows * slots
    share, lines = slots // many, prows // ncol
    cols = ncol * pcols
    bands = max(1, 128 // slots) * slots
    while n % bands:
        bands -= slots
    unit = max(1, min(lines, 128 // (cols * slots)))
    while lines % unit:
        unit -= 1
    rblock = cols * unit * slots
    rw, cw = HR * HD, HC * HD
    bf16, f32 = jnp.bfloat16, jnp.float32
    vmem = pltpu.VMEM
    dma = pltpu.SemaphoreType.DMA
    sizes = (nband, nrow, ncol, prows, pcols, slots, counts.shape[0])
    anywhere = pl.BlockSpec(memory_space=pltpu.HBM)
    return pl.pallas_call(
        functools.partial(kernel, sizes),
        out_shape=jax.ShapeDtypeStruct(tokens.shape, bf16),
        in_specs=[anywhere] * 8,
        out_specs=anywhere,
        scratch_shapes=[
            vmem((pcols, prows, slots, width), bf16),
            vmem(w_band_qkv.shape, bf16),
            vmem(w_band_out.shape, bf16),
            vmem(w_space_qkv.shape, bf16),
            vmem(w_space_out.shape, bf16),
            vmem((pcols, n, width), f32),
            vmem((n, 3 * HB * HD), bf16),
            vmem((n, HB * HD), bf16),
            vmem((n, n), bf16),
            vmem((n, n), bf16),
            vmem((bands, bands), f32),
            vmem((rblock, rblock), f32),
            vmem((pcols, many, share * prows, 3 * cw), bf16),
            vmem((pcols, many, share * prows, 3 * cw), bf16),
            vmem((pcols, many, share * prows, cw), bf16),
            vmem((pcols, many, share * prows, cw), bf16),
            vmem((pcols, ncol, lines * slots, 3 * rw), bf16),
            vmem((cols, lines * slots, 3 * rw), bf16),
            vmem((cols, lines * slots, rw), bf16),
            vmem((ncol, pcols, lines * slots, rw), bf16),
            vmem((pcols, prows, slots, width), bf16),
            pltpu.SMEM(counts.shape, jnp.int32),
            vmem(norm_band.shape, bf16),
            vmem(norm_space.shape, bf16),
            dma((pcols + 7,)),
            dma((pcols,)),
            dma((pcols, many)),
            dma((pcols, many)),
            dma((pcols, many)),
            dma((pcols, many)),
            dma((pcols, ncol)),
            dma((pcols, ncol)),
            dma((ncol,)),
            dma((ncol,)),
        ],
        compiler_params=pltpu.CompilerParams(
            collective_id=0, has_side_effects=True, vmem_limit_bytes=LIMIT
        ),
        cost_estimate=pl.CostEstimate(
            flops=12 * prows * pcols * slots * width * width // 2,
            bytes_accessed=12 * 1024 * 1024,
            transcendentals=4 * 1024 * 1024,
        ),
    )(
        counts,
        norm_band,
        norm_space,
        tokens,
        w_band_qkv,
        w_band_out,
        w_space_qkv,
        w_space_out,
    )


def solution(mesh):
    sizes = tuple(mesh.shape[a] for a in ("band", "row", "col"))
    placed = (P(("band", "row"), "col", None, None), P(), P(), P(), P(), P(), P(), P())
    return jax.shard_map(
        functools.partial(local, sizes),
        mesh=mesh,
        in_specs=placed,
        out_specs=P(("band", "row"), "col", None, None),
        check_vma=False,
    )
```
